32 devices in a mesh: dp: 8 (over z, x), fsdp: 4 (over y, core).
Axes of the slice: x: 2, y: 2, z: 4, core: 2. Of those that a mesh axis runs over, the one named last changes fastest.
Arguments:
- tokens: bfloat16 [65536, 768], P(('dp', 'fsdp')), may hold values from -6 to 6
- norm_gain: bfloat16 [768], P(('dp', 'fsdp')), may hold values from 0.099609375 to 1.8984375
- in_weight: bfloat16 [768, 3352], P(('dp', 'fsdp')), may hold values from -0.21875 to 0.21875
- conv_weight: bfloat16 [4, 1792], P(None, ('dp', 'fsdp')), may hold values from -3 to 3
- conv_bias: bfloat16 [1792], P(('dp', 'fsdp')), may hold values from -3 to 3
- decay_log: float32 [24], replicated, may hold values from 0 to 2.77
- step_bias: float32 [24], replicated, may hold values from -6.9 to -2.3
- skip_gain: float32 [24], replicated, may hold values from 0.5 to 1.5
- gate_gain: bfloat16 [1536], P(('dp', 'fsdp')), may hold values from 0.099609375 to 1.8984375
- out_weight: bfloat16 [1536, 768], P(('dp', 'fsdp')), may hold values from -0.15625 to 0.15625
- span_start: int32 [256], P(('dp', 'fsdp')), may hold values from 0 to 1, as said below
- span_valid: int32 [256], P(('dp', 'fsdp')), may hold values from 1 to 256, as said below
- cotangent: bfloat16 [65536, 768], P(('dp', 'fsdp')), may hold values from -6 to 6
Outputs:
- output: bfloat16 [65536, 768], P(('dp', 'fsdp'))
- tokens_grad: bfloat16 [65536, 768], P(('dp', 'fsdp'))
- norm_gain_grad: float32 [768], P(('dp', 'fsdp'))
- in_weight_grad: float32 [768, 3352], P(('dp', 'fsdp'))
- conv_weight_grad: float32 [4, 1792], P(None, ('dp', 'fsdp'))
- conv_bias_grad: float32 [1792], P(('dp', 'fsdp'))
- decay_log_grad: float32 [24], replicated
- step_bias_grad: float32 [24], replicated
- skip_gain_grad: float32 [24], replicated
- gate_gain_grad: float32 [1536], P(('dp', 'fsdp'))
- out_weight_grad: float32 [1536, 768], P(('dp', 'fsdp'))
The draws below stay inside these ranges and needn't reach their ends.
Inputs may be any that keep to these rules, and one draw needn't show every extreme that they name: `span_start`: each device's first span begins a sequence, so a sequence's spans lie on one device; the first device holds a single sequence over all its 8 spans. `span_valid`: every span but a sequence's last holds 256 live tokens; a sequence's last span holds 1 to 256.
All inputs are finite; a program needn't handle non-finite values.
Results may differ from the reference program's by a relative error of at most 0.008.
Values may be sent and summed in bfloat16 or wider, within the bound.
A program may use at most 320 MiB of HBM per device.

```python
import jax
import jax.numpy as jnp
from jax import lax

D = 768
CONV = 4
SPAN = 256
CH_DEV = 8
INNER = 1536
HEADS = 24
CONVCH = 1792
PROJ = 3352
TOK_DEV = 2048
NCHUNK = 256
TOKENS = 65536
DEVICES = 32


def span_layout(key):
    index = jnp.arange(NCHUNK, dtype=jnp.int32)
    place = index % CH_DEV
    coins = jax.random.randint(jax.random.fold_in(key, 11), (NCHUNK,), 0, 4)
    begins = jnp.where(place == 0, 1, jnp.where(index < CH_DEV, 0, jnp.where(coins == 0, 1, 0))).astype(jnp.int32)
    ending = jnp.concatenate([begins[1:], jnp.ones((1,), jnp.int32)])
    tails = jax.random.randint(jax.random.fold_in(key, 12), (NCHUNK,), 1, SPAN + 1)
    filled = jnp.where(jnp.logical_and(ending == 1, index >= CH_DEV), tails, SPAN).astype(jnp.int32)
    return (begins, filled)


def draw_span_start(key, part):
    begins, filled = span_layout(key)
    return begins


def draw_span_valid(key, part):
    begins, filled = span_layout(key)
    return filled


def level_of(rng, extent, cuts, smallest, high):
    def one(axis_at, blocks):
        steps = jax.random.uniform(jax.random.fold_in(jax.random.fold_in(rng, 6), axis_at), (blocks,), jnp.float32, smallest / len(cuts), high / len(cuts))
        return jnp.repeat(jnp.exp(steps), extent[axis_at] // blocks).reshape((-1,) + (1,) * (len(extent) - axis_at - 1))

    gain = one(*cuts[0])
    for cut in cuts[1:]:
        gain = gain * one(*cut)
    return gain


def centred(own_key, extent, scale, most, split=(), held_as=jnp.bfloat16):
    level = level_of(own_key, extent, split, -0.22, 0.18) if split else 1.0
    values = jax.random.normal(own_key, extent, jnp.float32) * scale * level
    return jnp.minimum(jnp.maximum(values, -most), most).astype(held_as)


def setup_inputs(seed: int = 0) -> dict:
    splits = jax.random.split(jax.random.key(seed), 14)
    tokens = centred(splits[0], (TOKENS, D), 1.0, 6.0, ((0, 32),))
    norm_gain = jnp.clip(1.0 + 0.18 * jax.random.normal(splits[1], (D,), jnp.float32), 0.099609375, 1.8984375).astype(jnp.bfloat16)
    in_weight = centred(splits[2], (D, PROJ), D ** -0.5, 0.21875, ((0, 32),))
    conv_weight = centred(splits[3], (CONV, CONVCH), CONV ** -0.5, 3.0, ((1, 32),))
    conv_bias = centred(splits[4], (CONVCH,), 0.3, 3.0, ((0, 32),))
    decay_log = jnp.clip(jax.random.uniform(splits[5], (HEADS,), jnp.float32, 0.0, 2.77), 0.0, 2.77)
    step_bias = jnp.clip(jax.random.uniform(splits[6], (HEADS,), jnp.float32, -6.9, -2.3), -6.9, -2.3)
    skip_gain = jnp.clip(jax.random.uniform(splits[7], (HEADS,), jnp.float32, 0.5, 1.5), 0.5, 1.5)
    gate_gain = jnp.clip(1.0 + 0.18 * jax.random.normal(splits[8], (INNER,), jnp.float32), 0.099609375, 1.8984375).astype(jnp.bfloat16)
    out_weight = centred(splits[9], (INNER, D), INNER ** -0.5, 0.15625, ((0, 32),))
    span_start = draw_span_start(jax.random.fold_in(splits[13], 71), 0)
    span_valid = draw_span_valid(jax.random.fold_in(splits[13], 71), 0)
    cotangent = centred(splits[12], (TOKENS, D), 1.0, 6.0, ((0, 32),))
    return {"tokens": tokens, "norm_gain": norm_gain, "in_weight": in_weight, "conv_weight": conv_weight, "conv_bias": conv_bias, "decay_log": decay_log, "step_bias": step_bias, "skip_gain": skip_gain, "gate_gain": gate_gain, "out_weight": out_weight, "span_start": span_start, "span_valid": span_valid, "cotangent": cotangent}


precise = lax.Precision.HIGHEST
epsilon = 1e-05

@jax.custom_vjp
def low(v):
    return lax.optimization_barrier(v.astype(jnp.bfloat16)).astype(jnp.float32)

@jax.custom_vjp
def low_back(v):
    return v

def low_keep(v):
    return (low(v), None)

def low_pass(kept, grad):
    return (grad,)

def back_keep(v):
    return (v, None)

def back_low(kept, grad):
    return (low(grad),)
low.defvjp(low_keep, low_pass)
low_back.defvjp(back_keep, back_low)

def rms_scale(values):
    return values * lax.rsqrt(lax.optimization_barrier(jnp.mean(values * values, axis=-1, keepdims=True)) + epsilon)

def causal_conv(signal, conv_taps, conv_shift, span_start):
    spans = signal.shape[0]
    length = signal.shape[1]
    width = signal.shape[2]
    tap_count = conv_taps.shape[0]
    flat = signal.reshape(spans * length, width)
    offsets = jnp.arange(length, dtype=jnp.int32)
    total = conv_shift[None, None, :] + conv_taps[tap_count - 1][None, None, :] * signal
    for shift_by in range(1, tap_count):
        moved = jnp.concatenate([jnp.zeros((shift_by, width), jnp.float32), flat[:-shift_by]], axis=0)
        moved = moved.reshape(spans, length, width)
        allowed = jnp.logical_or(offsets[None, :] >= shift_by, span_start[:, None] == 0).astype(jnp.float32)
        total = total + conv_taps[tap_count - 1 - shift_by][None, None, :] * moved * allowed[:, :, None]
    return total

def span_scan(values, step_sizes, rates, into_state, read_state, span_start):
    length = values.shape[1]
    heads = values.shape[2]
    head_dim = values.shape[3]
    running = jnp.cumsum(jnp.swapaxes(step_sizes * rates[None, None, :], 1, 2), axis=2)
    weighted = values * step_sizes[:, :, :, None]
    offsets = jnp.arange(length, dtype=jnp.int32)
    lower = (offsets[:, None] >= offsets[None, :])[None, None, :, :]
    spread = running[:, :, :, None] - running[:, :, None, :]
    within = jnp.where(lower, jnp.exp(jnp.where(lower, spread, 0.0)), 0.0)
    intersections = jnp.einsum('cin,cjn->cij', read_state, into_state, precision=precise)
    mixing = within * intersections[:, None, :, :]
    inside = jnp.einsum('chij,cjhp->cihp', mixing, weighted, precision=precise)
    leaving = jnp.exp(running[:, :, -1:] - running)
    deposits = jnp.einsum('chj,cjn,cjhp->chpn', leaving, into_state, weighted, precision=precise)
    carried = jnp.exp(running[:, :, -1])

    def advance(state, pieces):
        begin, deposit, factor = pieces
        entering = jnp.where(begin == 1, jnp.zeros_like(state), state)
        return (factor[:, None, None] * entering + deposit, entering)
    initial = jnp.zeros((heads, head_dim, into_state.shape[-1]), jnp.float32)
    final_state, entering = lax.scan(advance, initial, (span_start, deposits, carried))
    outside = jnp.einsum('cin,chpn,chi->cihp', read_state, entering, jnp.exp(running), precision=precise)
    return inside + outside

def mixer(projected, conv_taps, conv_shift, decay_log, step_bias, skip_gain, gate_gain, span_start):
    spans = projected.shape[0]
    length = projected.shape[1]
    inner = gate_gain.shape[0]
    channels = conv_shift.shape[0]
    state_width = (channels - inner) // 2
    heads = decay_log.shape[0]
    head_dim = inner // heads
    gate_part = projected[:, :, :inner]
    conv_part = projected[:, :, inner:inner + channels]
    step_part = projected[:, :, inner + channels:]
    convolved = jax.nn.silu(causal_conv(conv_part, conv_taps, conv_shift, span_start))
    values = convolved[:, :, :inner].reshape(spans, length, heads, head_dim)
    into_state = convolved[:, :, inner:inner + state_width]
    read_state = convolved[:, :, inner + state_width:]
    step_sizes = jax.nn.softplus(step_part + step_bias[None, None, :])
    rates = -jnp.exp(decay_log)
    scanned = span_scan(values, step_sizes, rates, into_state, read_state, span_start)
    scanned = scanned + skip_gain[None, None, :, None] * values
    mixed = scanned.reshape(spans, length, inner) * jax.nn.silu(gate_part)
    return rms_scale(mixed) * gate_gain

def forward_block(weights, block_tokens, block_start, block_live):
    norm_gain, in_weight, conv_taps, conv_shift, decay_log, step_bias, skip_gain, gate_gain, out_weight = weights
    spans = block_start.shape[0]
    normed = low(rms_scale(block_tokens) * norm_gain)
    projected = low_back(jnp.dot(normed, in_weight, precision=precise, preferred_element_type=jnp.float32))
    gated = mixer(projected.reshape(spans, -1, projected.shape[1]), conv_taps, conv_shift, decay_log, step_bias, skip_gain, gate_gain, block_start)
    gated = low(gated.reshape(block_tokens.shape[0], -1))
    branch = low_back(jnp.dot(gated, out_weight, precision=precise, preferred_element_type=jnp.float32))
    return block_tokens + branch * block_live[:, None]

def reference(tokens, norm_gain, in_weight, conv_weight, conv_bias, decay_log, step_bias, skip_gain, gate_gain, out_weight, span_start, span_valid, cotangent):
    offsets = jnp.arange(SPAN, dtype=jnp.int32)
    live = (offsets[None, :] < span_valid[:, None]).astype(jnp.float32).reshape(DEVICES, TOK_DEV)
    starts = span_start.reshape(DEVICES, CH_DEV)
    weights = (norm_gain.astype(jnp.float32), in_weight.astype(jnp.float32), conv_weight.astype(jnp.float32), conv_bias.astype(jnp.float32), decay_log.astype(jnp.float32), step_bias.astype(jnp.float32), skip_gain.astype(jnp.float32), gate_gain.astype(jnp.float32), out_weight.astype(jnp.float32))

    def whole(params, rows):
        rounded = (params[0], low(params[1]), params[2], params[3], params[4], params[5], params[6], params[7], low(params[8]))

        def step(carry, pieces):
            return (carry, jax.checkpoint(forward_block)(rounded, pieces[0], pieces[1], pieces[2]))
        carry, blocks = lax.scan(step, jnp.zeros((), jnp.float32), (rows.reshape(DEVICES, TOK_DEV, D), starts, live))
        return blocks.reshape(TOKENS, D)
    result, backward = jax.vjp(whole, weights, tokens.astype(jnp.float32))
    weight_grads, token_grads = backward(cotangent.astype(jnp.float32))
    return (result.astype(jnp.bfloat16), token_grads.astype(jnp.bfloat16), weight_grads[0], weight_grads[1], weight_grads[2], weight_grads[3], weight_grads[4], weight_grads[5], weight_grads[6], weight_grads[7], weight_grads[8])
```

```python
import jax
import jax.numpy as jnp
from jax import lax
from jax.experimental import pallas as pl
from jax.experimental.pallas import tpu as pltpu
from jax.sharding import PartitionSpec as P

epsilon = 1e-05
f32 = jnp.float32
bf16 = jnp.bfloat16
Q = 128
PAD = 128
AXES = ("dp", "fsdp")


def mm(a, b, ca=1, cb=0):
    return lax.dot_general(a, b, (((ca,), (cb,)), ((), ())), preferred_element_type=f32)


def split2(v):
    hi = v.astype(bf16)
    return hi, (v - hi.astype(f32)).astype(bf16)


def spread_heads(v, heads_map):
    hi, lo = split2(v)
    return mm(hi, heads_map) + mm(lo, heads_map)


def sum_heads(v, heads_map):
    hi, lo = split2(v)
    return mm(hi, heads_map, 1, 1) + mm(lo, heads_map, 1, 1)


def tri_sum(tri, v):
    hi = v.astype(bf16)
    rest = v - hi.astype(f32)
    mid = rest.astype(bf16)
    low = (rest - mid.astype(f32)).astype(bf16)
    return mm(tri, hi) + mm(tri, mid) + mm(tri, low)


def sigmoid(v):
    return 1.0 / (1.0 + jnp.exp(-v))


def softplus(v):
    return jnp.maximum(v, 0.0) + jnp.log1p(jnp.exp(-jnp.abs(v)))


def forward_kernel(
    start_ref, tokens_ref, bgrad_ref, w_ref, wstep_ref, wout_ref, gain_ref, taps_ref, bias_ref,
    rates_ref, sbias_ref, skip_ref, ggain_ref, map_ref,
    normed_ref, gated_ref, dgate_ref, dy_ref, rs_ref, pre_ref, cpart_ref, sraw_ref, state_out_ref,
    ggrad_ref, skipgrad_ref,
    ext, state, ybuf,
):
    inner = ggain_ref.shape[1]
    chans = bias_ref.shape[1]
    nstate = (chans - inner) // 2
    pairs = inner // 128
    step = pl.program_id(0)
    per = pl.num_programs(0) // start_ref.shape[0]
    fresh = jnp.logical_and(step % per == 0, start_ref[step // per] == 1)

    @pl.when(step == 0)
    def _():
        ggrad_ref[...] = jnp.zeros_like(ggrad_ref)
        skipgrad_ref[...] = jnp.zeros_like(skipgrad_ref)

    @pl.when(jnp.logical_or(fresh, step == 0))
    def _():
        state[...] = jnp.zeros_like(state)
        ext[0:8, :] = jnp.zeros((8, chans), f32)

    rows = tokens_ref[...].astype(f32)
    r = lax.rsqrt(jnp.mean(rows * rows, axis=1, keepdims=True) + epsilon)
    normed = (rows * r * gain_ref[...]).astype(bf16)
    normed_ref[...] = normed
    heads_map = map_ref[...]
    cpart = mm(normed, w_ref[:, inner : inner + chans])
    cpart_ref[...] = cpart.astype(bf16)
    ext[8:, :] = cpart
    pre = bias_ref[...] + taps_ref[3:4, :] * cpart
    for j in range(3):
        pre = pre + taps_ref[j : j + 1, :] * ext[5 + j : 5 + j + Q, :]
    ext[0:8, :] = ext[Q : Q + 8, :]
    pre_ref[...] = pre
    conv = pre * sigmoid(pre)
    x = conv[:, :inner]
    b = conv[:, inner : inner + nstate]
    c = conv[:, inner + nstate :]
    b16 = b.astype(bf16)
    c16 = c.astype(bf16)
    sraw = mm(normed, wstep_ref[...]) + sbias_ref[...]
    sraw_ref[...] = sraw
    dt = softplus(sraw)
    ri = lax.broadcasted_iota(jnp.int32, (Q, Q), 0)
    ci = lax.broadcasted_iota(jnp.int32, (Q, Q), 1)
    lower = ri >= ci
    run = tri_sum(jnp.where(lower, 1.0, 0.0).astype(bf16), dt * rates_ref[...])
    run_t = run.T
    w = x * spread_heads(dt, heads_map)
    w16 = w.astype(bf16)
    er = spread_heads(jnp.exp(run), heads_map)
    leaving = spread_heads(jnp.exp(run[Q - 1 : Q, :] - run), heads_map)
    lw16 = (leaving * w16.astype(f32)).astype(bf16)
    inter = mm(c16, b16, 1, 1)
    left = lax.broadcasted_iota(jnp.int32, (Q, 128), 1) < 64
    zero16 = jnp.zeros((Q, 128), bf16)
    state16 = state[...].astype(bf16)
    state_out_ref[0] = state16
    ybuf[...] = mm(c16, state16) * er
    for k in range(pairs):
        mats = []
        for h in (2 * k, 2 * k + 1):
            seg = run[:, h : h + 1] - run_t[h : h + 1, :]
            e = jnp.exp(jnp.where(lower, seg, -1e30))
            mats.append((e * inter).astype(bf16))
        wp = w16[:, 128 * k : 128 * k + 128]
        rhs = jnp.concatenate([jnp.where(left, wp, zero16), jnp.where(left, zero16, wp)], axis=0)
        ybuf[:, 128 * k : 128 * k + 128] += mm(jnp.concatenate(mats, axis=1), rhs)
    state[...] = er[Q - 1 : Q, :] * state[...] + mm(b.T.astype(bf16), lw16)

    y = ybuf[...]
    gate = mm(normed, w_ref[:, :inner])
    ggrad = mm(bgrad_ref[...], wout_ref[...], 1, 1)
    scanned = y + skip_ref[...] * x
    sg = sigmoid(gate)
    sil = gate * sg
    m = scanned * sil
    r2 = lax.rsqrt(jnp.mean(m * m, axis=1, keepdims=True) + epsilon)
    u = m * r2
    gated_ref[...] = (u * ggain_ref[...]).astype(bf16)
    ggrad_ref[...] += jnp.sum(ggrad * u, axis=0, keepdims=True)
    g = ggrad * ggain_ref[...]
    dm = r2 * (g - u * jnp.mean(g * u, axis=1, keepdims=True))
    dgate_ref[...] = (dm * scanned * (sg * (1.0 + gate * (1.0 - sg)))).astype(bf16)
    dsc = dm * sil
    skipgrad_ref[...] += jnp.sum(dsc * x, axis=0, keepdims=True)
    dy16 = dsc.astype(bf16)
    dy_ref[...] = dy16
    rs_ref[...] = sum_heads(dy16.astype(f32) * y, heads_map)


def backward_kernel(
    start_ref, dy_ref, rs_ref, pre_ref, cpart_ref, sraw_ref, state_in_ref, taps_ref, rates_ref,
    skip_ref, map_ref,
    dcs_ref, dtaps_ref, dbias_ref, ddecay_ref, dstep_ref,
    ext, dstate, dwbuf,
):
    inner = skip_ref.shape[1]
    chans = taps_ref.shape[1]
    nstate = (chans - inner) // 2
    pairs = inner // 128
    heads = dcs_ref.shape[1] - chans
    step = pl.program_id(0)
    steps = pl.num_programs(0)
    at = steps - 1 - step
    per = steps // start_ref.shape[0]
    fresh = jnp.logical_and(at % per == 0, start_ref[at // per] == 1)

    @pl.when(step == 0)
    def _():
        dtaps_ref[...] = jnp.zeros_like(dtaps_ref)
        dbias_ref[...] = jnp.zeros_like(dbias_ref)
        ddecay_ref[...] = jnp.zeros_like(ddecay_ref)
        dstep_ref[...] = jnp.zeros_like(dstep_ref)
        dstate[...] = jnp.zeros_like(dstate)
        ext[Q:, :] = jnp.zeros((8, chans), f32)

    heads_map = map_ref[...]
    pre = pre_ref[...]
    sgm = sigmoid(pre)
    conv = pre * sgm
    x = conv[:, :inner]
    b = conv[:, inner : inner + nstate]
    c = conv[:, inner + nstate :]
    b16 = b.astype(bf16)
    c16 = c.astype(bf16)
    sraw = sraw_ref[...]
    dt = softplus(sraw)
    rates = rates_ref[...]
    ri = lax.broadcasted_iota(jnp.int32, (Q, Q), 0)
    ci = lax.broadcasted_iota(jnp.int32, (Q, Q), 1)
    upper = ci >= ri
    run = tri_sum(jnp.where(ri >= ci, 1.0, 0.0).astype(bf16), dt * rates)
    run_t = run.T
    dt_e = spread_heads(dt, heads_map)
    w16 = (x * dt_e).astype(bf16)
    wf = w16.astype(f32)
    er = spread_heads(jnp.exp(run), heads_map)
    leaving = spread_heads(jnp.exp(run[Q - 1 : Q, :] - run), heads_map)
    lw16 = (leaving * wf).astype(bf16)
    inter_t = mm(b16, c16, 1, 1)
    dy16 = dy_ref[...]
    dy = dy16.astype(f32)
    ds = dstate[...]
    ds16 = ds.astype(bf16)
    s16 = state_in_ref[0]
    left = lax.broadcasted_iota(jnp.int32, (Q, 128), 1) < 64
    zero16 = jnp.zeros((Q, 128), bf16)
    dinter_t = jnp.zeros((Q, Q), f32)
    for k in range(pairs):
        wp = w16[:, 128 * k : 128 * k + 128]
        dyp = dy16[:, 128 * k : 128 * k + 128]
        both_w = jnp.concatenate([jnp.where(left, wp, zero16), jnp.where(left, zero16, wp)], axis=0)
        dmt = mm(both_w, dyp, 1, 1)
        mats = []
        for n in range(2):
            h = 2 * k + n
            seg = run_t[h : h + 1, :] - run[:, h : h + 1]
            e = jnp.exp(jnp.where(upper, seg, -1e30))
            mats.append((e * inter_t).astype(bf16))
            dinter_t = dinter_t + dmt[n * Q : n * Q + Q, :] * e
        rhs = jnp.concatenate([jnp.where(left, dyp, zero16), jnp.where(left, zero16, dyp)], axis=0)
        dwbuf[:, 128 * k : 128 * k + 128] = mm(jnp.concatenate(mats, axis=1), rhs)
    dey16 = (dy * er).astype(bf16)
    dep = leaving * mm(b16, ds16)
    dw = dwbuf[...] + dep
    db = mm(dinter_t.astype(bf16), c16) + mm(lw16, ds16, 1, 1)
    dc = mm(dinter_t.T.astype(bf16), b16) + mm(dey16, s16, 1, 1)
    carried = er[Q - 1 : Q, :]
    end = jnp.sum(wf * dep, axis=0, keepdims=True) + carried * jnp.sum(
        s16.astype(f32) * ds, axis=0, keepdims=True
    )
    end = sum_heads(jnp.broadcast_to(end, (8, inner)), heads_map)[0:1, :]
    keep = jnp.where(fresh, 0.0, 1.0)
    dstate[...] = (carried * ds + mm(c.T.astype(bf16), dey16)) * keep
    drun = rs_ref[...] - sum_heads(wf * dw, heads_map)
    da = tri_sum(jnp.where(upper, 1.0, 0.0).astype(bf16), drun) + end
    ddt = da * rates + sum_heads(dw * x, heads_map)
    ddecay_ref[...] += jnp.sum(da * dt * rates, axis=0, keepdims=True)
    dsr = ddt * sigmoid(sraw)
    dstep_ref[...] += jnp.sum(dsr, axis=0, keepdims=True)
    dcs_ref[:, chans:] = dsr[:, :heads].astype(bf16)
    dx = dw * dt_e + skip_ref[...] * dy
    dsilu = sgm * (1.0 + pre * (1.0 - sgm))
    ext[0:Q, :inner] = dx * dsilu[:, :inner]
    ext[0:Q, inner : inner + nstate] = db * dsilu[:, inner : inner + nstate]
    ext[0:Q, inner + nstate :] = dc * dsilu[:, inner + nstate :]
    cpart = cpart_ref[...].astype(f32)
    dcp = jnp.zeros((Q, chans), f32)
    for s in range(4):
        moved = ext[s : s + Q, :]
        if s == 0:
            dbias_ref[...] += jnp.sum(moved, axis=0, keepdims=True)
        dcp = dcp + taps_ref[3 - s : 4 - s, :] * moved
        dtaps_ref[3 - s : 4 - s, :] += jnp.sum(cpart * moved, axis=0, keepdims=True)
    dcs_ref[:, :chans] = dcp.astype(bf16)
    ext[Q:, :] = ext[0:8, :] * keep


def whole(shape):
    return pl.BlockSpec(shape, lambda i: (0,) * len(shape))


def run_forward(start, tokens, bgrad, w, wstep, wout, gain, taps, bias, rates, sbias, skip, ggain, heads_map):
    count, width = tokens.shape
    inner = ggain.shape[1]
    chans = bias.shape[1]
    nstate = (chans - inner) // 2
    steps = count // Q

    def rowblock(n):
        return pl.BlockSpec((Q, n), lambda i: (i, 0))

    consts = (w, wstep, wout, gain, taps, bias, rates, sbias, skip, ggain, heads_map)
    sds = jax.ShapeDtypeStruct
    return pl.pallas_call(
        forward_kernel,
        grid=(steps,),
        in_specs=[pl.BlockSpec(memory_space=pltpu.SMEM), rowblock(width), rowblock(width)]
        + [whole(v.shape) for v in consts],
        out_specs=[
            rowblock(width), rowblock(inner), rowblock(inner), rowblock(inner), rowblock(PAD),
            rowblock(chans), rowblock(chans), rowblock(PAD),
            pl.BlockSpec((1, nstate, inner), lambda i: (i, 0, 0)),
            whole((1, inner)), whole((1, inner)),
        ],
        out_shape=[
            sds((count, width), bf16), sds((count, inner), bf16), sds((count, inner), bf16),
            sds((count, inner), bf16), sds((count, PAD), f32), sds((count, chans), f32),
            sds((count, chans), bf16), sds((count, PAD), f32), sds((steps, nstate, inner), bf16),
            sds((1, inner), f32), sds((1, inner), f32),
        ],
        scratch_shapes=[
            pltpu.VMEM((Q + 8, chans), f32), pltpu.VMEM((nstate, inner), f32), pltpu.VMEM((Q, inner), f32),
        ],
        compiler_params=pltpu.CompilerParams(
            dimension_semantics=("arbitrary",), vmem_limit_bytes=56 * 1024 * 1024
        ),
        cost_estimate=pl.CostEstimate(flops=30_000_000_000, bytes_accessed=80_000_000, transcendentals=20_000_000),
        name="mixer_forward",
    )(start, tokens, bgrad, *consts)


def run_backward(start, dy, rs, pre, cpart, sraw, states, taps, rates, skip, heads_map, heads):
    count, inner = dy.shape
    chans = pre.shape[1]
    nstate = states.shape[1]
    steps = count // Q

    def rowblock(n):
        return pl.BlockSpec((Q, n), lambda i: (steps - 1 - i, 0))

    consts = (taps, rates, skip, heads_map)
    sds = jax.ShapeDtypeStruct
    return pl.pallas_call(
        backward_kernel,
        grid=(steps,),
        in_specs=[
            pl.BlockSpec(memory_space=pltpu.SMEM), rowblock(inner), rowblock(PAD), rowblock(chans),
            rowblock(chans), rowblock(PAD),
            pl.BlockSpec((1, nstate, inner), lambda i: (steps - 1 - i, 0, 0)),
        ]
        + [whole(v.shape) for v in consts],
        out_specs=[
            rowblock(chans + heads), whole((4, chans)), whole((1, chans)), whole((1, PAD)), whole((1, PAD)),
        ],
        out_shape=[
            sds((count, chans + heads), bf16), sds((4, chans), f32), sds((1, chans), f32),
            sds((1, PAD), f32), sds((1, PAD), f32),
        ],
        scratch_shapes=[
            pltpu.VMEM((Q + 8, chans), f32), pltpu.VMEM((nstate, inner), f32), pltpu.VMEM((Q, inner), f32),
        ],
        compiler_params=pltpu.CompilerParams(
            dimension_semantics=("arbitrary",), vmem_limit_bytes=56 * 1024 * 1024
        ),
        cost_estimate=pl.CostEstimate(flops=30_000_000_000, bytes_accessed=60_000_000, transcendentals=20_000_000),
        name="mixer_backward",
    )(start, dy, rs, pre, cpart, sraw, states, *consts)


def local_mixer(tokens, bgrad, w, wout, gain, taps, bias, decay_log, step_bias, skip_gain, ggain, start):
    inner = ggain.shape[0]
    chans = bias.shape[0]
    heads = decay_log.shape[0]
    lane = jnp.arange(inner, dtype=jnp.int32) // (inner // heads)
    heads_map = (jnp.arange(PAD, dtype=jnp.int32)[:, None] == lane[None, :]).astype(bf16)

    def padded(v):
        return jnp.pad(v, (0, PAD - heads))[None, :]

    rates = padded(-jnp.exp(decay_log))
    skip = jnp.repeat(skip_gain, inner // heads)[None, :]
    wstep = jnp.pad(w[:, inner + chans : inner + chans + heads], ((0, 0), (0, PAD - heads)))
    taps = taps.astype(f32)
    bias = bias.astype(f32)[None, :]
    normed, gated, dgate, dy, rs, pre, cpart, sraw, states, ggrad, skipgrad = run_forward(
        start, tokens, bgrad, w, wstep, wout, gain.astype(f32)[None, :], taps, bias, rates,
        padded(step_bias), skip, ggain.astype(f32)[None, :], heads_map,
    )
    dcs, dtaps, dbias, ddecay, dstep = run_backward(
        start, dy, rs, pre, cpart, sraw, states, taps, rates, skip, heads_map, heads
    )
    skip_grad = skipgrad.reshape(heads, -1).sum(axis=1)
    return normed, gated, dgate, dcs, dtaps, dbias[0], ddecay[0, :heads], dstep[0, :heads], skip_grad, ggrad[0]


def per_device(
    tokens, norm_gain, in_weight, conv_weight, conv_bias, decay_log, step_bias, skip_gain, gate_gain,
    out_weight, span_start, span_valid, cotangent,
):
    spans = span_start.shape[0]
    length = tokens.shape[0] // spans
    offsets = jnp.arange(length, dtype=jnp.int32)
    live = (offsets[None, :] < span_valid[:, None]).astype(f32).reshape(-1, 1)
    wrows, proj = in_weight.shape
    smalls = [norm_gain, conv_weight.reshape(-1), conv_bias, gate_gain]
    total = sum(v.shape[0] for v in smalls)
    extra = -(-total // wrows)
    extra = -(-extra // 8) * 8
    flat = jnp.concatenate(smalls + [jnp.zeros((extra * wrows - total,), bf16)])
    joined = jnp.concatenate([in_weight, flat.reshape(wrows, extra)], axis=1)
    full_w = lax.all_gather(joined, AXES, axis=0, tiled=True)
    full_out = lax.all_gather(out_weight, AXES, axis=0, tiled=True)
    small = full_w[:, proj:].reshape(-1, extra * wrows)
    edges = [0]
    for v in smalls:
        edges.append(edges[-1] + v.shape[0])
    full_norm = small[:, edges[0] : edges[1]].reshape(-1)
    devices = small.shape[0]
    full_taps = small[:, edges[1] : edges[2]].reshape(devices, conv_weight.shape[0], -1)
    full_taps = full_taps.transpose(1, 0, 2).reshape(conv_weight.shape[0], -1)
    full_bias = small[:, edges[2] : edges[3]].reshape(-1)
    full_gate = small[:, edges[3] : edges[4]].reshape(-1)
    inner = full_gate.shape[0]

    flowing = cotangent.astype(f32)
    branch_grad = (flowing * live).astype(bf16)
    (normed, gated, dgate, dcs, taps_grad, bias_grad, decay_grad, step_grad, skip_grad, gain_grad) = local_mixer(
        tokens, branch_grad, full_w, full_out, full_norm, full_taps, full_bias, decay_log, step_bias,
        skip_gain, full_gate, span_start,
    )
    scatter = lambda v, dim=0: lax.psum_scatter(v, AXES, scatter_dimension=dim, tiled=True)
    out_share = scatter(mm(gated, branch_grad, 0, 0))
    gate_share = scatter(mm(normed, dgate, 0, 0))
    rest_share = scatter(mm(normed, dcs, 0, 0))
    normed_grad = mm(dgate, full_w[:, :inner], 1, 1) + mm(dcs, full_w[:, inner:proj], 1, 1)
    rows = tokens.astype(f32)
    r = lax.rsqrt(jnp.mean(rows * rows, axis=1, keepdims=True) + epsilon)
    u = rows * r
    norm_grad = jnp.sum(normed_grad * u, axis=0)
    g = normed_grad * full_norm.astype(f32)[None, :]
    token_grad = (flowing + r * (g - u * jnp.mean(g * u, axis=1, keepdims=True))).astype(bf16)
    branch = mm(gated, full_out)
    output = (rows + branch * live).astype(bf16)
    head_sums = lax.psum((decay_grad, step_grad, skip_grad), AXES)
    return (
        output,
        token_grad,
        scatter(norm_grad),
        jnp.concatenate([gate_share, rest_share], axis=1),
        scatter(taps_grad, 1),
        scatter(bias_grad),
        head_sums[0],
        head_sums[1],
        head_sums[2],
        scatter(gain_grad),
        out_share,
    )


def solution(mesh):
    rows = P(AXES, None)
    vec = P(AXES)
    cols = P(None, AXES)
    in_specs = (rows, vec, rows, cols, vec, P(), P(), P(), vec, rows, vec, vec, rows)
    out_specs = (rows, rows, vec, rows, cols, vec, P(), P(), P(), vec, rows)
    return jax.shard_map(
        per_device, mesh=mesh, in_specs=in_specs, out_specs=out_specs, check_vma=False
    )
```
